1024 devices in a mesh: expert: 16 (over y, x), tensor: 64 (over z, core).
Axes of the slice: x: 4, y: 4, z: 32, core: 2. Of those that a mesh axis runs over, the one named last changes fastest.
Arguments:
- tokens: bfloat16 [2048, 7168], P('expert', 'tensor'), may hold values from -6 to 6
- gate_weights: bfloat16 [2048, 1], P('expert'), may hold values from 0.099609375 to 1
- expert_ids: int32 [2048, 1], P('expert'), may hold values from 0 to 15; in each aligned block of 128 rows (0 to 127, 128 to 255, ...) at most 12 rows name the same one
- w_gate: bfloat16 [16, 7168, 2048], P('expert', 'tensor'), may hold values from -0.0625 to 0.0625
- w_up: bfloat16 [16, 7168, 2048], P('expert', 'tensor'), may hold values from -0.0625 to 0.0625
- w_down: bfloat16 [16, 2048, 7168], P('expert', None, 'tensor'), may hold values from -0.125 to 0.125
- grad_out: bfloat16 [2048, 7168], P('expert', 'tensor'), may hold values from -6 to 6
Outputs:
- mixed: bfloat16 [2048, 7168], P('expert', 'tensor')
- grad_tokens: bfloat16 [2048, 7168], P('expert', 'tensor')
- grad_w_gate: bfloat16 [16, 7168, 2048], P('expert', 'tensor')
- grad_w_up: bfloat16 [16, 7168, 2048], P('expert', 'tensor')
- grad_w_down: bfloat16 [16, 2048, 7168], P('expert', None, 'tensor')
The draws below stay inside these ranges and needn't reach their ends.
Inputs may be any that keep to these rules, and one draw needn't show every extreme that they name: `expert_ids`: the 1 expert of a token differ. The tokens of one expert index (aligned blocks of 128 rows) name one expert at most 12 times, a bound that some block reaches.
All inputs are finite; a program needn't handle non-finite values.
Results may differ from the reference program's by a relative error of at most 0.0058.
Values may be sent and summed in bfloat16 or wider, within the bound.
A program may use at most 32 MiB of HBM per device.

```python
import math
import jax
import jax.numpy as jnp
import numpy as np
from jax import lax

D = 7168
FF = 2048
TOPK = 1
TOK_G = 128
EXPERTS = 16
SLOT = 12
ROWS = 192
TOKENS = 2048


def block_levels(own_key, dims, split, low, top_value):
    def one(position, parts):
        draws = jax.random.uniform(jax.random.fold_in(jax.random.fold_in(own_key, 6), position), (parts,), jnp.float32, low / len(split), top_value / len(split))
        return jnp.repeat(jnp.exp(draws), dims[position] // parts).reshape((-1,) + (1,) * (len(dims) - position - 1))

    level = one(*split[0])
    for cut in split[1:]:
        level = level * one(*cut)
    return level


def routed_block(rng, own, number, rows, count, top, bound, lean):
    sequence = jax.random.permutation(rng, count)
    heavy_load, common = portions_of(count, rows * top, bound, lean, True), portions_of(count, rows * top, bound, lean, False)
    places = jnp.arange(count)

    def named(tallies, offset_by):
        used = int((tallies > 0).sum())
        fixed = max(1, used // 4)
        passed = fixed + (places - fixed + offset_by * (used - fixed)) % max(1, count - fixed)
        return jnp.zeros((count,), jnp.int32).at[sequence[jnp.where(places < fixed, places, passed)]].set(jnp.asarray(tallies, jnp.int32))

    tallies = jnp.where(number % 4 == 0, named(heavy_load, number // 4), named(common, number - number // 4 - 1))
    mixed = jax.random.permutation(jax.random.fold_in(own, 3), count)
    donor, sink = mixed[0:count // 2 * 2:2], mixed[1:count // 2 * 2:2]
    margin = jnp.minimum(tallies[donor] - 1, bound - tallies[sink]) // 2
    margin = jnp.where((donor == sequence[0]) | (sink == sequence[0]) | (tallies[sink] == 0), 0, jnp.maximum(margin, 0))
    passed = jax.random.randint(jax.random.fold_in(own, 4), (count // 2,), 0, 1 << 20) % (margin + 1)
    tallies = tallies.at[donor].add(-passed).at[sink].add(passed)
    items = jnp.searchsorted(jnp.cumsum(tallies), jnp.arange(rows * top), side="right").astype(jnp.int32)
    table = items.reshape(top, rows).T
    table = table[jax.random.permutation(jax.random.fold_in(own, 1), rows)]
    offset_by = jax.random.randint(jax.random.fold_in(own, 2), (rows, 1), 0, top)
    return jnp.take_along_axis(table, (jnp.arange(top)[None, :] + offset_by) % top, axis=1)


def portions_of(count, total, most, slope, full):
    loads = [(1 << 20) // math.isqrt(grade ** slope) + 1 for grade in range(1, count + 1)]
    largest = most if full else min(most, max(-(-total // count), total * loads[0] // sum(loads)))
    least = 1 if total - largest >= count - 1 else 0
    holding, surplus = [largest] + [least] * (count - 1), total - largest - least * (count - 1)
    while surplus > 0:
        free = [i for i in range(1, count) if holding[i] < largest] or [i for i in range(1, count) if holding[i] < most]
        whole, left = sum([loads[i] for i in free]), surplus
        for i in free:
            addition = min(most - holding[i], max(1, left * loads[i] // whole), surplus)
            holding[i] = holding[i] + addition
            surplus = surplus - addition
    return np.array(holding)


def scatter_about(rng, dims, width, reach, cuts=(), kind=jnp.bfloat16):
    values = jax.random.normal(rng, dims, jnp.float32) * width
    if len(cuts) > 0:
        values = block_levels(rng, dims, cuts, -0.22, 0.18) * values
    return jnp.clip(values, min=-reach, max=reach).astype(kind)


def setup_inputs(seed: int = 0) -> dict:
    key_list = jax.random.split(jax.random.key(seed), 8)
    tokens = scatter_about(key_list[0], (TOKENS, D), 1.0, 6.0, ((0, 16), (1, 64)))
    gate_weights = jnp.clip(0.099609375 + 0.9003906 * jax.random.uniform(key_list[1], (TOKENS, TOPK), jnp.float32) ** block_levels(key_list[1], (TOKENS, TOPK), ((0, 16),), -0.2, 0.2), 0.099609375, 1.0).astype(jnp.bfloat16)
    expert_ids_keys = jax.random.split(jax.random.fold_in(key_list[2], 1), TOKENS // TOK_G)
    expert_ids_turns = jax.random.permutation(jax.random.fold_in(key_list[2], 3), TOKENS // TOK_G)
    expert_ids = jax.vmap(lambda own, number: routed_block(jax.random.fold_in(key_list[2], 2), own, number, TOK_G, EXPERTS, TOPK, SLOT, 2))(expert_ids_keys, expert_ids_turns).reshape((TOKENS, TOPK))
    w_gate = scatter_about(key_list[3], (EXPERTS, D, FF), D ** -0.5, 0.0625, ((0, 16), (1, 64)))
    w_up = scatter_about(key_list[4], (EXPERTS, D, FF), D ** -0.5, 0.0625, ((0, 16), (1, 64)))
    w_down = scatter_about(key_list[5], (EXPERTS, FF, D), FF ** -0.5, 0.125, ((0, 16), (2, 64)))
    grad_out = scatter_about(key_list[6], (TOKENS, D), 1.0, 6.0, ((0, 16), (1, 64)))
    return dict(tokens=tokens, gate_weights=gate_weights, expert_ids=expert_ids, w_gate=w_gate, w_up=w_up, w_down=w_down, grad_out=grad_out)


def reference(tokens, gate_weights, expert_ids, w_gate, w_up, w_down, grad_out):
    flat_ids = expert_ids.reshape(-1).astype(jnp.int32)
    flat_gate = gate_weights.reshape(-1)
    route_token = (jnp.arange(flat_ids.shape[0], dtype=jnp.int32) // TOPK).astype(jnp.int32)

    def one_expert(packed):
        weight_gate, weight_up, weight_down, index = packed
        chosen = flat_ids == index
        picks = jnp.nonzero(chosen, size=ROWS, fill_value=0)[0].astype(jnp.int32)
        live = (jnp.arange(ROWS, dtype=jnp.int32) < jnp.sum(chosen.astype(jnp.int32))).astype(jnp.float32)
        token_index = route_token[picks]
        weight = flat_gate[picks].astype(jnp.float32) * live
        x_rows = tokens[token_index]
        gate = jnp.dot(x_rows, weight_gate, preferred_element_type=jnp.float32)
        up = jnp.dot(x_rows, weight_up, preferred_element_type=jnp.float32)
        sigma = jax.nn.sigmoid(gate)
        active = gate * sigma
        hidden = (active * up).astype(jnp.bfloat16)
        expert_out = jnp.dot(hidden, weight_down, preferred_element_type=jnp.float32).astype(jnp.bfloat16)
        scaled = (weight[:, None] * grad_out[token_index].astype(jnp.float32)).astype(jnp.bfloat16)
        d_hidden = jnp.dot(scaled, weight_down.T, preferred_element_type=jnp.float32)
        d_gate = (d_hidden * up * sigma * (1.0 + gate * (1.0 - sigma))).astype(jnp.bfloat16)
        d_up = (d_hidden * active).astype(jnp.bfloat16)
        route_grad = (jnp.dot(d_gate, weight_gate.T, preferred_element_type=jnp.float32)
                      + jnp.dot(d_up, weight_up.T, preferred_element_type=jnp.float32)).astype(jnp.bfloat16)
        grad_gate = jnp.dot(x_rows.T, d_gate, preferred_element_type=jnp.float32).astype(jnp.bfloat16)
        grad_up = jnp.dot(x_rows.T, d_up, preferred_element_type=jnp.float32).astype(jnp.bfloat16)
        grad_down = jnp.dot(hidden.T, scaled, preferred_element_type=jnp.float32).astype(jnp.bfloat16)
        return expert_out, route_grad, token_index, weight, live, grad_gate, grad_up, grad_down

    indices = jnp.arange(EXPERTS, dtype=jnp.int32)
    outs = lax.map(one_expert, (w_gate, w_up, w_down, indices))
    expert_out, route_grad, token_index, weight, live, grad_w_gate, grad_w_up, grad_w_down = outs
    flat_index = token_index.reshape(-1)
    mixed_terms = (weight[:, :, None] * expert_out.astype(jnp.float32)).reshape(-1, D)
    mixed = jax.ops.segment_sum(mixed_terms, flat_index, num_segments=TOKENS).astype(jnp.bfloat16)
    grad_terms = (live[:, :, None] * route_grad.astype(jnp.float32)).reshape(-1, D)
    grad_tokens = jax.ops.segment_sum(grad_terms, flat_index, num_segments=TOKENS).astype(jnp.bfloat16)
    return mixed, grad_tokens, grad_w_gate, grad_w_up, grad_w_down
```

```python
import functools

import jax
import jax.numpy as jnp
from jax import lax
from jax.experimental import pallas as pl
from jax.experimental.pallas import tpu as pltpu
from jax.sharding import PartitionSpec as P

MESH = pl.DeviceIdType.MESH
F32 = jnp.float32
BF16 = jnp.bfloat16
LANES = 128
FULL = 256
TAIL = 64
UNITS = 32
FOLD = UNITS + UNITS // 2
KINDS = 3
SENT = F32

NT = (((1,), (1,)), ((), ()))
NN = (((1,), (0,)), ((), ()))


def dot(a, b, dims=NN):
    return lax.dot_general(a, b, dims, preferred_element_type=F32)


def padded(x):
    return jnp.concatenate([x, jnp.zeros((LANES - x.shape[0], x.shape[1]), x.dtype)], axis=0)


def iota(shape, dim):
    return lax.broadcasted_iota(jnp.int32, shape, dim)


def kernel(
    experts, chips,
    tok_ref, g_ref, id_ref, wg_ref, wu_ref, wd_ref, dy_ref,
    mixed_ref, gtok_ref, gwg_ref, gwu_ref, gwd_ref,
    out_slots, in_slots, ret_slots, back_slots, xt, wt, wm, part, gath, acc_out, acc_back,
    disp_s, disp_r, ret_s, ret_r, mate_s, mate_r, rs_s, rs_r, ag_s, ag_r, am_s, am_r,
):
    e = lax.axis_index("expert")
    t = lax.axis_index("tensor")
    z, c = lax.div(t, 2), lax.rem(t, 2)
    pad = FULL // experts
    slot = 192 // experts
    depth = wg_ref.shape[0]
    half = chips // 2
    weights = (wg_ref, wu_ref, wd_ref)

    def at_chip(k):
        return lax.rem(k + 2 * chips, chips)

    up_id = {"tensor": 2 * at_chip(z + 1) + c}
    down_id = {"tensor": 2 * at_chip(z - 1) + c}
    mate_id = {"tensor": 2 * z + 1 - c}
    ring = (up_id, down_id)

    barrier = pltpu.get_barrier_semaphore()
    for peer in (up_id, down_id, mate_id):
        pl.semaphore_signal(barrier, inc=1, device_id=peer, device_id_type=MESH)

    def greet(i, _):
        pl.semaphore_signal(
            barrier, inc=1, device_id={"expert": lax.rem(e + i, experts)}, device_id_type=MESH
        )
        return 0

    lax.fori_loop(1, experts, greet, 0)

    ids = id_ref[...]
    here = (iota((experts, LANES), 0) == ids).astype(F32)
    before = (iota((LANES, LANES), 0) < iota((LANES, LANES), 1)).astype(BF16)
    ranks = dot(here.astype(BF16), before)
    position = jnp.sum(here * ranks, axis=0, keepdims=True)
    target = ids * pad + position.astype(jnp.int32)
    matched = iota((FULL, LANES), 0) == target
    place = jnp.where(matched, 1.0, 0.0).astype(BF16)
    weighted = jnp.where(matched, g_ref[...].astype(F32), 0.0).astype(BF16)
    x_slots = dot(place, padded(tok_ref[...]), NT).astype(BF16)
    dy_slots = dot(weighted, padded(dy_ref[...]), NT).astype(BF16)
    out_slots[:, :, :LANES] = x_slots.reshape(experts, pad, LANES)
    out_slots[:, :, LANES:] = dy_slots.reshape(experts, pad, LANES)

    pl.semaphore_wait(barrier, experts + 2)

    def leave(src, dst, send, recv, i):
        peer = lax.rem(e + i, experts)
        return pltpu.make_async_remote_copy(
            src_ref=src.at[peer], dst_ref=dst.at[e], send_sem=send.at[i], recv_sem=recv.at[i],
            device_id={"expert": peer}, device_id_type=MESH,
        )

    def arrive(src, dst, send, recv, i):
        origin = lax.rem(e - i + experts, experts)
        return pltpu.make_async_remote_copy(
            src_ref=src.at[origin], dst_ref=dst.at[origin], send_sem=send.at[i],
            recv_sem=recv.at[i], device_id={"expert": origin}, device_id_type=MESH,
        )

    def all_start(src, dst, send, recv):
        def body(i, _):
            leave(src, dst, send, recv, i).start()
            return 0

        lax.fori_loop(1, experts, body, 0)
        dst[e] = src[e]

    def all_wait(src, dst, send, recv):
        def body(i, _):
            arrive(src, dst, send, recv, i).wait_recv()
            return 0

        lax.fori_loop(1, experts, body, 0)

    def all_sent(src, dst, send, recv):
        def body(i, _):
            leave(src, dst, send, recv, i).wait_send()
            return 0

        lax.fori_loop(1, experts, body, 0)

    dispatch = (out_slots, in_slots, disp_s, disp_r)
    all_start(*dispatch)

    def mate_weights(k):
        return pltpu.make_async_remote_copy(
            src_ref=wt.at[k, :, 1 - c], dst_ref=wm.at[k], send_sem=mate_s.at[k],
            recv_sem=mate_r.at[k], device_id=mate_id, device_id_type=MESH,
        )

    for k in range(KINDS):
        def turn(i, _, k=k):
            cols = pl.ds(pl.multiple_of(i * LANES, LANES), LANES)
            block = padded(weights[k][:, cols]).T
            wt[k, pl.ds(2 * i, 2)] = block.reshape(2, 2, UNITS, LANES)
            return 0

        lax.fori_loop(0, chips // 2, turn, 0)
        mate_weights(k).start()

    s_i, r_i = iota((FULL, FULL), 0), iota((FULL, FULL), 1)
    inner = lax.bitwise_and(s_i, pad - 1)
    first = lax.shift_right_logical(s_i, pad.bit_length() - 1) * slot
    r_of = jnp.where(r_i >= 192, r_i - TAIL, r_i)
    valid = inner < slot
    spread = jnp.where(valid & (r_of - first == inner), 1.0, 0.0).astype(BF16)
    gather = jnp.where(valid & (r_i - first == inner), 1.0, 0.0).astype(BF16)

    all_wait(*dispatch)
    arrived = in_slots[...].reshape(FULL, FULL)
    panels = dot(arrived.T, spread).astype(BF16)
    xt[0, 0] = panels[:LANES]
    xt[1, 0] = panels[LANES:]
    mate_rows = pltpu.make_async_remote_copy(
        src_ref=xt.at[:, 0], dst_ref=xt.at[:, 1], send_sem=mate_s.at[KINDS],
        recv_sem=mate_r.at[KINDS], device_id=mate_id, device_id_type=MESH,
    )
    mate_rows.start()
    for k in range(KINDS):
        mate_weights(k).wait_recv()
    mate_rows.wait_recv()

    low = iota((UNITS // 2, LANES), 1) < TAIL

    def partial(chip):
        sums = []
        for k in range(KINDS):
            lhs = jnp.concatenate([wt[k, chip, c], wm[k, chip]], axis=1)
            r = dot(lhs, xt[0 if k < 2 else 1].reshape(FULL, FULL))
            tail = jnp.where(low, r[: UNITS // 2, LANES:], r[UNITS // 2 :, LANES:])
            sums.append(jnp.concatenate([r[:, :LANES], tail], axis=0))
        return sums

    def hop(way, s, k):
        return pltpu.make_async_remote_copy(
            src_ref=part.at[way, s, k], dst_ref=part.at[way, s + 1, k],
            send_sem=rs_s.at[way, s, k], recv_sem=rs_r.at[way, s, k],
            device_id=ring[way], device_id_type=MESH,
        )

    mine = partial(at_chip(z + half))
    for k in range(KINDS):
        part[0, 0, k] = mine[k].astype(SENT)
        hop(0, 0, k).start()
    mine = partial(at_chip(z - half + 1))
    for k in range(KINDS):
        part[1, 0, k] = mine[k].astype(SENT)
        hop(1, 0, k).start()

    def rs_step(i, _):
        ups = partial(at_chip(z + half - i))
        for k in range(KINDS):
            hop(0, i - 1, k).wait_recv()
            part[0, i, k] = (part[0, i, k].astype(F32) + ups[k]).astype(SENT)
            hop(0, i, k).start()

        @pl.when(i > 1)
        def _():
            downs = partial(at_chip(z - half + i))
            for k in range(KINDS):
                hop(1, i - 2, k).wait_recv()
                part[1, i - 1, k] = (part[1, i - 1, k].astype(F32) + downs[k]).astype(SENT)
                hop(1, i - 1, k).start()

        return 0

    lax.fori_loop(1, half, rs_step, 0)
    own = partial(z)
    total = []
    for k in range(KINDS):
        hop(0, half - 1, k).wait_recv()
        hop(1, half - 2, k).wait_recv()
        total.append(part[0, half, k].astype(F32) + part[1, half - 1, k].astype(F32) + own[k])
    gate, up, d_hidden = total
    sigma = jax.nn.sigmoid(gate)
    active = gate * sigma
    gath[z, c, 0] = (active * up).astype(BF16)
    gath[z, c, 1] = (d_hidden * up * sigma * (1.0 + gate * (1.0 - sigma))).astype(BF16)
    gath[z, c, 2] = (d_hidden * active).astype(BF16)

    def lap(way, s, k):
        origin = at_chip(z - s) if way == 0 else at_chip(z + s)
        return pltpu.make_async_remote_copy(
            src_ref=gath.at[origin, c, k], dst_ref=gath.at[origin, c, k],
            send_sem=ag_s.at[way, s, k], recv_sem=ag_r.at[way, s, k],
            device_id=ring[way], device_id_type=MESH,
        )

    def lap_in(way, s, k):
        origin = at_chip(z - s - 1) if way == 0 else at_chip(z + s + 1)
        return pltpu.make_async_remote_copy(
            src_ref=gath.at[origin, c, k], dst_ref=gath.at[origin, c, k],
            send_sem=ag_s.at[way, s, k], recv_sem=ag_r.at[way, s, k],
            device_id=ring[way], device_id_type=MESH,
        )

    def across(origin, k):
        return pltpu.make_async_remote_copy(
            src_ref=gath.at[origin, c, k], dst_ref=gath.at[origin, c, k],
            send_sem=am_s.at[origin, k], recv_sem=am_r.at[origin, k],
            device_id=mate_id, device_id_type=MESH,
        )

    def across_in(origin, k):
        return pltpu.make_async_remote_copy(
            src_ref=gath.at[origin, 1 - c, k], dst_ref=gath.at[origin, 1 - c, k],
            send_sem=am_s.at[origin, k], recv_sem=am_r.at[origin, k],
            device_id=mate_id, device_id_type=MESH,
        )

    for k in range(KINDS):
        lap(0, 0, k).start()
        lap(1, 0, k).start()
        across(z, k).start()

    acc_out[...] = jnp.zeros_like(acc_out)
    acc_back[...] = jnp.zeros_like(acc_back)
    odd = lax.rem(z, 2)
    low2 = iota((UNITS // 2, LANES), 1) < TAIL
    zero2 = jnp.zeros((UNITS // 2, LANES), BF16)

    def use(pair):
        first_chip = at_chip(z - odd + 2 * pair)
        for i in range(2):
            for k in range(KINDS):
                across_in(first_chip + i, k).wait_recv()
        panel = []
        for k in range(KINDS):
            rows = []
            for i in range(2):
                for core in range(2):
                    v = gath[first_chip + i, core, k]
                    tail = v[UNITS:]
                    rows.append(
                        jnp.concatenate(
                            [
                                v[:UNITS],
                                jnp.concatenate(
                                    [jnp.where(low2, tail, zero2), jnp.where(low2, zero2, tail)],
                                    axis=0,
                                ),
                            ],
                            axis=1,
                        )
                    )
            panel.append(jnp.concatenate(rows, axis=0))
        hidden, d_gate, d_up = panel
        cols = pl.ds(pl.multiple_of(first_chip * 2 * UNITS, LANES), LANES)
        acc_out[...] += dot(wd_ref[:, cols], hidden)
        acc_back[...] += dot(wg_ref[:, cols], d_gate) + dot(wu_ref[:, cols], d_up)
        x_panel, dy_panel = xt[0, 0][:depth], xt[1, 0][:depth]
        gwg_ref[:, cols] = dot(x_panel, d_gate, NT).astype(BF16)
        gwu_ref[:, cols] = dot(x_panel, d_up, NT).astype(BF16)
        gwd_ref[:, cols] = dot(dy_panel, hidden, NT).astype(BF16)

    def forward(s):
        for k in range(KINDS):
            lap_in(0, s, k).wait_recv()

            @pl.when(s < half - 1)
            def _():
                lap(0, s + 1, k).start()

            across(at_chip(z - s - 1), k).start()

            @pl.when(s < half - 1)
            def _():
                lap_in(1, s, k).wait_recv()

                @pl.when(s < half - 2)
                def _():
                    lap(1, s + 1, k).start()

                across(at_chip(z + s + 1), k).start()

    forward(0)
    forward(1)

    def ag_step(j, _):
        forward(2 * j)
        use(j - 1 + odd)
        forward(2 * j + 1)
        use(odd - j)
        return 0

    lax.fori_loop(1, half // 2, ag_step, 0)
    use(half // 2 - 1 + odd)
    use(odd - half // 2)

    def folded(acc):
        a = acc[:, LANES:]
        whole = jnp.concatenate([acc[:, :LANES], a + pltpu.roll(a, TAIL, 1)], axis=1)
        return padded(whole.astype(BF16))

    out_rows = dot(gather, folded(acc_out[...]), NT).astype(BF16)
    ret_slots[:, :, :LANES] = out_rows.reshape(experts, pad, LANES)
    back_rows = dot(gather, folded(acc_back[...]), NT).astype(BF16)
    ret_slots[:, :, LANES:] = back_rows.reshape(experts, pad, LANES)
    homeward = (ret_slots, back_slots, ret_s, ret_r)
    all_start(*homeward)

    all_sent(*dispatch)
    for k in range(KINDS):
        mate_weights(k).wait_send()
    mate_rows.wait_send()

    def drain(s, _):
        for k in range(KINDS):
            hop(0, s, k).wait_send()
            lap(0, s, k).wait_send()

            @pl.when(s < half - 1)
            def _():
                hop(1, s, k).wait_send()
                lap(1, s, k).wait_send()

        return 0

    lax.fori_loop(0, half, drain, 0)

    def drain_across(o, _):
        for k in range(KINDS):
            across(o, k).wait_send()
        return 0

    lax.fori_loop(0, chips, drain_across, 0)

    all_wait(*homeward)
    returned = back_slots[...].reshape(FULL, FULL).T
    mixed_ref[...] = dot(returned[:depth], weighted).astype(BF16)
    gtok_ref[...] = dot(returned[LANES : LANES + depth], place).astype(BF16)
    all_sent(*homeward)


def local(experts, chips, tokens, gate_weights, expert_ids, w_gate, w_up, w_down, grad_out):
    depth, width = w_gate.shape[1:]
    pad = FULL // experts
    half = chips // 2
    dma = pltpu.SemaphoreType.DMA
    slots = pltpu.VMEM((experts, pad, FULL), BF16)
    rows = jax.ShapeDtypeStruct((depth, LANES), BF16)
    grads = jax.ShapeDtypeStruct((depth, width), BF16)
    vmem = pl.BlockSpec(memory_space=pltpu.VMEM)
    mixed, grad_tokens, gwg, gwu, gwd = pl.pallas_call(
        functools.partial(kernel, experts, chips),
        out_shape=(rows, rows, grads, grads, grads),
        in_specs=[vmem] * 7,
        out_specs=(vmem,) * 5,
        scratch_shapes=[
            slots, slots, slots, slots,
            pltpu.VMEM((2, 2, LANES, FULL), BF16),
            pltpu.VMEM((KINDS, chips, 2, UNITS, LANES), BF16),
            pltpu.VMEM((KINDS, chips, UNITS, LANES), BF16),
            pltpu.VMEM((2, half + 1, KINDS, FOLD, LANES), SENT),
            pltpu.VMEM((chips, 2, KINDS, FOLD, LANES), BF16),
            pltpu.VMEM((depth, FULL), F32),
            pltpu.VMEM((depth, FULL), F32),
            dma((experts,)), dma((experts,)), dma((experts,)), dma((experts,)),
            dma((KINDS + 1,)), dma((KINDS + 1,)),
            dma((2, half, KINDS)), dma((2, half, KINDS)),
            dma((2, half, KINDS)), dma((2, half, KINDS)),
            dma((chips, KINDS)), dma((chips, KINDS)),
        ],
        compiler_params=pltpu.CompilerParams(
            collective_id=0, has_side_effects=True, vmem_limit_bytes=40 * 2**20
        ),
        name="routed_experts",
    )(tokens.T, gate_weights.T, expert_ids.T, w_gate[0], w_up[0], w_down[0].T, grad_out.T)
    return mixed.T, grad_tokens.T, gwg[None], gwu[None], gwd.T[None]


def solution(mesh):
    in_specs = (
        P("expert", "tensor"),
        P("expert", None),
        P("expert", None),
        P("expert", "tensor", None),
        P("expert", "tensor", None),
        P("expert", None, "tensor"),
        P("expert", "tensor"),
    )
    out_specs = (
        P("expert", "tensor"),
        P("expert", "tensor"),
        P("expert", "tensor", None),
        P("expert", "tensor", None),
        P("expert", None, "tensor"),
    )
    body = functools.partial(local, mesh.shape["expert"], mesh.shape["tensor"] // 2)
    return jax.shard_map(body, mesh=mesh, in_specs=in_specs, out_specs=out_specs, check_vma=False)
```

```python
import functools

import jax
import jax.numpy as jnp
from jax import lax
from jax.experimental import pallas as pl
from jax.experimental.pallas import tpu as pltpu
from jax.sharding import PartitionSpec as P

MESH = pl.DeviceIdType.MESH
F32 = jnp.float32
BF16 = jnp.bfloat16
LANES = 128
FULL = 256
TAIL = 64
UNITS = 32
FOLD = UNITS + UNITS // 2
KINDS = 3
FAR = 12
NEAR = 7
SUMS = ((0, 4, -8, -1), (1, 4, -16, 1), (1, 4, 8, 1), (0, 3, 15, -1), (0, 7, 7, -1), (1, 7, -7, 1))
LAPS = ((0, 7, 0, -1), (1, 7, 0, 1), (0, 4, -12, -1), (1, 4, -12, 1), (0, 4, 12, -1), (1, 3, 12, 1))

NT = (((1,), (1,)), ((), ()))
NN = (((1,), (0,)), ((), ()))


def dot(a, b, dims=NN):
    return lax.dot_general(a, b, dims, preferred_element_type=F32)


def padded(x):
    return jnp.concatenate([x, jnp.zeros((LANES - x.shape[0], x.shape[1]), x.dtype)], axis=0)


def iota(shape, dim):
    return lax.broadcasted_iota(jnp.int32, shape, dim)


def kernel(
    experts, chips,
    tok_ref, g_ref, id_ref, wg_hbm, wu_hbm, wd_hbm, dy_ref,
    mixed_ref, gtok_ref, gwg_ref, gwu_ref, gwd_ref,
    wg_ref, wu_ref, wd_ref,
    out_slots, in_slots, ret_slots, back_slots, xt, wt, wm, part, far_out, far_in, gath, acc_out, acc_back,
    disp_s, disp_r, ret_s, ret_r, mate_s, mate_r, rs_s, rs_r, far_s, far_r, ag_s, ag_r, ax_s, ax_r, am_s, am_r,
    load_s,
):
    e = lax.axis_index("expert")
    t = lax.axis_index("tensor")
    z, c = lax.div(t, 2), lax.rem(t, 2)
    pad = FULL // experts
    slot = 192 // experts
    depth = wg_ref.shape[0]
    weights = (wg_ref, wu_ref, wd_ref)
    loads = [
        pltpu.make_async_copy(src, dst, load_s.at[k])
        for k, (src, dst) in enumerate(zip((wg_hbm, wu_hbm, wd_hbm), weights))
    ]
    for load in loads:
        load.start()

    def at_chip(k):
        return lax.rem(k + 2 * chips, chips)

    up_id = {"tensor": 2 * at_chip(z + 1) + c}
    down_id = {"tensor": 2 * at_chip(z - 1) + c}
    mate_id = {"tensor": 2 * z + 1 - c}
    ring = (up_id, down_id)
    far_ids = ({"tensor": 2 * at_chip(z + FAR) + c}, {"tensor": 2 * at_chip(z - FAR) + c})

    barrier = pltpu.get_barrier_semaphore()
    for peer in (up_id, down_id, mate_id, *far_ids):
        pl.semaphore_signal(barrier, inc=1, device_id=peer, device_id_type=MESH)

    def greet(i, _):
        pl.semaphore_signal(
            barrier, inc=1, device_id={"expert": lax.rem(e + i, experts)}, device_id_type=MESH
        )
        return 0

    lax.fori_loop(1, experts, greet, 0)

    ids = id_ref[...]
    here = (iota((experts, LANES), 0) == ids).astype(F32)
    before = (iota((LANES, LANES), 0) < iota((LANES, LANES), 1)).astype(BF16)
    ranks = dot(here.astype(BF16), before)
    position = jnp.sum(here * ranks, axis=0, keepdims=True)
    target = ids * pad + position.astype(jnp.int32)
    matched = iota((FULL, LANES), 0) == target
    place = jnp.where(matched, 1.0, 0.0).astype(BF16)
    weighted = jnp.where(matched, g_ref[...].astype(F32), 0.0).astype(BF16)
    x_slots = dot(place, padded(tok_ref[...]), NT).astype(BF16)
    dy_slots = dot(weighted, padded(dy_ref[...]), NT).astype(BF16)
    out_slots[:, :, :LANES] = x_slots.reshape(experts, pad, LANES)
    out_slots[:, :, LANES:] = dy_slots.reshape(experts, pad, LANES)

    pl.semaphore_wait(barrier, experts + 4)

    def leave(src, dst, send, recv, i):
        peer = lax.rem(e + i, experts)
        return pltpu.make_async_remote_copy(
            src_ref=src.at[peer], dst_ref=dst.at[e], send_sem=send.at[i], recv_sem=recv.at[i],
            device_id={"expert": peer}, device_id_type=MESH,
        )

    def arrive(src, dst, send, recv, i):
        origin = lax.rem(e - i + experts, experts)
        return pltpu.make_async_remote_copy(
            src_ref=src.at[origin], dst_ref=dst.at[origin], send_sem=send.at[i],
            recv_sem=recv.at[i], device_id={"expert": origin}, device_id_type=MESH,
        )

    def all_start(src, dst, send, recv):
        def body(i, _):
            leave(src, dst, send, recv, i).start()
            return 0

        lax.fori_loop(1, experts, body, 0)
        dst[e] = src[e]

    def all_wait(src, dst, send, recv):
        def body(i, _):
            arrive(src, dst, send, recv, i).wait_recv()
            return 0

        lax.fori_loop(1, experts, body, 0)

    def all_sent(src, dst, send, recv):
        def body(i, _):
            leave(src, dst, send, recv, i).wait_send()
            return 0

        lax.fori_loop(1, experts, body, 0)

    dispatch = (out_slots, in_slots, disp_s, disp_r)
    all_start(*dispatch)

    def mate_weights(k):
        return pltpu.make_async_remote_copy(
            src_ref=wt.at[k, :, 1 - c], dst_ref=wm.at[k], send_sem=mate_s.at[k],
            recv_sem=mate_r.at[k], device_id=mate_id, device_id_type=MESH,
        )

    for k in range(KINDS):
        def turn(i, _, k=k):
            cols = pl.ds(pl.multiple_of(i * LANES, LANES), LANES)
            block = padded(weights[k][:, cols]).T
            wt[k, pl.ds(2 * i, 2)] = block.reshape(2, 2, UNITS, LANES)
            return 0

        loads[k].wait()
        lax.fori_loop(0, chips // 2, turn, 0)
        mate_weights(k).start()

    s_i, r_i = iota((FULL, FULL), 0), iota((FULL, FULL), 1)
    inner = lax.bitwise_and(s_i, pad - 1)
    first = lax.shift_right_logical(s_i, pad.bit_length() - 1) * slot
    r_of = jnp.where(r_i >= 192, r_i - TAIL, r_i)
    valid = inner < slot
    spread = jnp.where(valid & (r_of - first == inner), 1.0, 0.0).astype(BF16)
    gather = jnp.where(valid & (r_i - first == inner), 1.0, 0.0).astype(BF16)

    all_wait(*dispatch)
    arrived = in_slots[...].reshape(FULL, FULL)
    panels = dot(arrived.T, spread).astype(BF16)
    xt[0, 0] = panels[:LANES]
    xt[1, 0] = panels[LANES:]
    mate_rows = pltpu.make_async_remote_copy(
        src_ref=xt.at[:, 0], dst_ref=xt.at[:, 1], send_sem=mate_s.at[KINDS],
        recv_sem=mate_r.at[KINDS], device_id=mate_id, device_id_type=MESH,
    )
    mate_rows.start()
    for k in range(KINDS):
        mate_weights(k).wait_recv()
    mate_rows.wait_recv()

    low = iota((UNITS // 2, LANES), 1) < TAIL

    def partial(chip):
        sums = []
        for k in range(KINDS):
            lhs = jnp.concatenate([wt[k, chip, c], wm[k, chip]], axis=1)
            r = dot(lhs, xt[0 if k < 2 else 1].reshape(FULL, FULL))
            tail = jnp.where(low, r[: UNITS // 2, LANES:], r[UNITS // 2 :, LANES:])
            sums.append(jnp.concatenate([r[:, :LANES], tail], axis=0))
        return sums

    def hop(i, s, k):
        return pltpu.make_async_remote_copy(
            src_ref=part.at[i, s, k], dst_ref=part.at[i, s + 1, k],
            send_sem=rs_s.at[i, s, k], recv_sem=rs_r.at[i, s, k],
            device_id=ring[SUMS[i][0]], device_id_type=MESH,
        )

    def summed(i, s):
        return partial(at_chip(z + SUMS[i][2] + SUMS[i][3] * s))

    def far(h, k):
        return pltpu.make_async_remote_copy(
            src_ref=far_out.at[h, k], dst_ref=far_in.at[h, k],
            send_sem=far_s.at[h, k], recv_sem=far_r.at[h, k],
            device_id=far_ids[h], device_id_type=MESH,
        )

    for i in range(len(SUMS)):
        mine = summed(i, 0)
        for k in range(KINDS):
            part[i, 0, k] = mine[k]
            hop(i, 0, k).start()

    def advance(i, s):
        mine = summed(i, s)
        for k in range(KINDS):
            hop(i, s - 1, k).wait_recv()
            part[i, s, k] += mine[k]
            hop(i, s, k).start()

    def rs_step(s, _):
        for i in range(len(SUMS)):
            if SUMS[i][1] > 3:
                advance(i, s)
            else:
                pl.when(s < SUMS[i][1])(functools.partial(advance, i, s))
        return 0

    lax.fori_loop(1, 4, rs_step, 0)
    for h, (one, two) in enumerate(((2, 3), (0, 1))):
        mine = partial(at_chip(z + FAR - 2 * FAR * h))
        for k in range(KINDS):
            for i in (one, two):
                hop(i, SUMS[i][1] - 1, k).wait_recv()
            far_out[h, k] = (
                part[one, SUMS[one][1], k] + part[two, SUMS[two][1], k] + mine[k]
            ).astype(BF16)
            far(h, k).start()

    def rs_late(s, _):
        advance(4, s)
        advance(5, s)
        return 0

    lax.fori_loop(4, NEAR, rs_late, 0)
    own = partial(z)
    total = []
    for k in range(KINDS):
        hop(4, NEAR - 1, k).wait_recv()
        hop(5, NEAR - 1, k).wait_recv()
        total.append(part[4, NEAR, k] + part[5, NEAR, k] + own[k])
    for k in range(KINDS):
        for h in range(2):
            far(h, k).wait_recv()
            total[k] += far_in[h, k].astype(F32)
    gate, up, d_hidden = total
    sigma = jax.nn.sigmoid(gate)
    active = gate * sigma
    gath[z, c, 0] = (active * up).astype(BF16)
    gath[z, c, 1] = (d_hidden * up * sigma * (1.0 + gate * (1.0 - sigma))).astype(BF16)
    gath[z, c, 2] = (d_hidden * active).astype(BF16)

    def lap(i, s, k):
        origin = at_chip(z + LAPS[i][2] + LAPS[i][3] * s)
        return pltpu.make_async_remote_copy(
            src_ref=gath.at[origin, c, k], dst_ref=gath.at[origin, c, k],
            send_sem=ag_s.at[i, s, k], recv_sem=ag_r.at[i, s, k],
            device_id=ring[LAPS[i][0]], device_id_type=MESH,
        )

    def lap_from(i, s):
        return at_chip(z - 1 + 2 * LAPS[i][0] + LAPS[i][2] + LAPS[i][3] * s)

    def lap_in(i, s, k):
        origin = lap_from(i, s)
        return pltpu.make_async_remote_copy(
            src_ref=gath.at[origin, c, k], dst_ref=gath.at[origin, c, k],
            send_sem=ag_s.at[i, s, k], recv_sem=ag_r.at[i, s, k],
            device_id=ring[LAPS[i][0]], device_id_type=MESH,
        )

    def leap(h, k, arriving):
        origin = at_chip(z - FAR + 2 * FAR * h) if arriving else z
        return pltpu.make_async_remote_copy(
            src_ref=gath.at[origin, c, k], dst_ref=gath.at[origin, c, k],
            send_sem=ax_s.at[h, k], recv_sem=ax_r.at[h, k],
            device_id=far_ids[h], device_id_type=MESH,
        )

    def across(origin):
        return pltpu.make_async_remote_copy(
            src_ref=gath.at[origin, c], dst_ref=gath.at[origin, c],
            send_sem=am_s.at[origin], recv_sem=am_r.at[origin],
            device_id=mate_id, device_id_type=MESH,
        )

    def across_in(origin):
        return pltpu.make_async_remote_copy(
            src_ref=gath.at[origin, 1 - c], dst_ref=gath.at[origin, 1 - c],
            send_sem=am_s.at[origin], recv_sem=am_r.at[origin],
            device_id=mate_id, device_id_type=MESH,
        )

    for k in range(KINDS):
        leap(0, k, False).start()
        leap(1, k, False).start()
        lap(0, 0, k).start()
        lap(1, 0, k).start()
    across(z).start()

    acc_out[...] = jnp.zeros_like(acc_out)
    acc_back[...] = jnp.zeros_like(acc_back)
    odd = lax.rem(z, 2)
    low2 = iota((UNITS // 2, LANES), 1) < TAIL
    zero2 = jnp.zeros((UNITS // 2, LANES), BF16)

    def use(pair):
        first_chip = at_chip(z - odd + 2 * pair)
        for i in range(2):
            across_in(first_chip + i).wait_recv()
        panel = []
        for k in range(KINDS):
            rows = []
            for i in range(2):
                for core in range(2):
                    v = gath[first_chip + i, core, k]
                    tail = v[UNITS:]
                    rows.append(
                        jnp.concatenate(
                            [
                                v[:UNITS],
                                jnp.concatenate(
                                    [jnp.where(low2, tail, zero2), jnp.where(low2, zero2, tail)],
                                    axis=0,
                                ),
                            ],
                            axis=1,
                        )
                    )
            panel.append(jnp.concatenate(rows, axis=0))
        hidden, d_gate, d_up = panel
        cols = pl.ds(pl.multiple_of(first_chip * 2 * UNITS, LANES), LANES)
        acc_out[...] += dot(wd_ref[:, cols], hidden)
        acc_back[...] += dot(wg_ref[:, cols], d_gate) + dot(wu_ref[:, cols], d_up)
        x_panel, dy_panel = xt[0, 0][:depth], xt[1, 0][:depth]
        gwg_ref[:, cols] = dot(x_panel, d_gate, NT).astype(BF16)
        gwu_ref[:, cols] = dot(x_panel, d_up, NT).astype(BF16)
        gwd_ref[:, cols] = dot(dy_panel, hidden, NT).astype(BF16)

    def forward(i, s):
        last = LAPS[i][1] - 1
        for k in range(KINDS):
            lap_in(i, s, k).wait_recv()

            @pl.when(s < last)
            def _():
                lap(i, s + 1, k).start()

        across(lap_from(i, s)).start()

    def use_all(pairs):
        def body(i, _):
            pair = pairs[-1]
            for j in range(len(pairs) - 1):
                pair = jnp.where(i == j, pairs[j], pair)
            use(pair)
            return 0

        lax.fori_loop(0, len(pairs), body, 0)

    def near_step(s, _):
        forward(0, s)
        forward(1, s)
        return 0

    lax.fori_loop(0, 3, near_step, 0)
    use_all((0, 1, -1))
    for h in range(2):
        for k in range(KINDS):
            leap(h, k, True).wait_recv()
            lap(2 + 2 * h, 0, k).start()
            lap(3 + 2 * h, 0, k).start()
        across(at_chip(z - FAR + 2 * FAR * h)).start()

    def ag_step(s):
        forward(0, s + 3)
        forward(1, s + 3)
        for i in range(2, len(LAPS)):
            if s < LAPS[i][1]:
                forward(i, s)

    ag_step(0)
    use_all((6, -6))
    ag_step(1)
    use_all((2, -2))
    ag_step(2)
    use_all((5, -5, 7, -7, 6 * odd - 3))
    ag_step(3)
    use_all((3 - 6 * odd, 4, -4, -8))

    def folded(acc):
        a = acc[:, LANES:]
        whole = jnp.concatenate([acc[:, :LANES], a + pltpu.roll(a, TAIL, 1)], axis=1)
        return padded(whole.astype(BF16))

    out_rows = dot(gather, folded(acc_out[...]), NT).astype(BF16)
    ret_slots[:, :, :LANES] = out_rows.reshape(experts, pad, LANES)
    back_rows = dot(gather, folded(acc_back[...]), NT).astype(BF16)
    ret_slots[:, :, LANES:] = back_rows.reshape(experts, pad, LANES)
    homeward = (ret_slots, back_slots, ret_s, ret_r)
    all_start(*homeward)

    all_sent(*dispatch)
    for k in range(KINDS):
        mate_weights(k).wait_send()
    mate_rows.wait_send()

    for h in range(2):
        for k in range(KINDS):
            far(h, k).wait_send()
            leap(h, k, False).wait_send()
    for chains, sent in ((SUMS, hop), (LAPS, lap)):
        for i in range(len(chains)):
            def drain(s, _, i=i, sent=sent):
                for k in range(KINDS):
                    sent(i, s, k).wait_send()
                return 0

            lax.fori_loop(0, chains[i][1], drain, 0)

    def drain_across(o, _):
        across(o).wait_send()
        return 0

    lax.fori_loop(0, chips, drain_across, 0)

    all_wait(*homeward)
    returned = back_slots[...].reshape(FULL, FULL).T
    mixed_ref[...] = dot(returned[:depth], weighted).astype(BF16)
    gtok_ref[...] = dot(returned[LANES : LANES + depth], place).astype(BF16)
    all_sent(*homeward)


def hand_on(*refs):
    for src, dst in zip(refs[:5], refs[5:]):
        dst[...] = src[...]


def local(experts, chips, tokens, gate_weights, expert_ids, w_gate, w_up, w_down, grad_out):
    depth, width = w_gate.shape[1:]
    pad = FULL // experts
    dma = pltpu.SemaphoreType.DMA
    slots = pltpu.VMEM((experts, pad, FULL), BF16)
    rows = jax.ShapeDtypeStruct((depth, LANES), BF16)
    grads = jax.ShapeDtypeStruct((depth, width), BF16)
    vmem = pl.BlockSpec(memory_space=pltpu.VMEM)
    results = pl.pallas_call(
        functools.partial(kernel, experts, chips),
        out_shape=(rows, rows, grads, grads, grads),
        in_specs=[vmem] * 3 + [pl.BlockSpec(memory_space=pl.ANY)] * 3 + [vmem],
        out_specs=(vmem,) * 5,
        scratch_shapes=[
            pltpu.VMEM((depth, width), BF16),
            pltpu.VMEM((depth, width), BF16),
            pltpu.VMEM((depth, width), BF16),
            slots, slots, slots, slots,
            pltpu.VMEM((2, 2, LANES, FULL), BF16),
            pltpu.VMEM((KINDS, chips, 2, UNITS, LANES), BF16),
            pltpu.VMEM((KINDS, chips, UNITS, LANES), BF16),
            pltpu.VMEM((len(SUMS), NEAR + 1, KINDS, FOLD, LANES), F32),
            pltpu.VMEM((2, KINDS, FOLD, LANES), BF16),
            pltpu.VMEM((2, KINDS, FOLD, LANES), BF16),
            pltpu.VMEM((chips, 2, KINDS, FOLD, LANES), BF16),
            pltpu.VMEM((depth, FULL), F32),
            pltpu.VMEM((depth, FULL), F32),
            dma((experts,)), dma((experts,)), dma((experts,)), dma((experts,)),
            dma((KINDS + 1,)), dma((KINDS + 1,)),
            dma((len(SUMS), NEAR, KINDS)), dma((len(SUMS), NEAR, KINDS)),
            dma((2, KINDS)), dma((2, KINDS)),
            dma((len(LAPS), NEAR, KINDS)), dma((len(LAPS), NEAR, KINDS)),
            dma((2, KINDS)), dma((2, KINDS)),
            dma((chips,)), dma((chips,)),
            dma((KINDS,)),
        ],
        compiler_params=pltpu.CompilerParams(
            collective_id=0, has_side_effects=True, vmem_limit_bytes=56 * 2**20
        ),
        name="routed_experts",
    )(tokens.T, gate_weights.T, expert_ids.T, w_gate[0], w_up[0], w_down[0].T, grad_out.T)
    mixed, grad_tokens, gwg, gwu, gwd = pl.pallas_call(
        hand_on,
        out_shape=(rows, rows, grads, grads, grads),
        in_specs=[vmem] * 5,
        out_specs=(vmem,) * 5,
        name="hand_on",
    )(*results)
    return mixed.T, grad_tokens.T, gwg[None], gwu[None], gwd.T[None]


def solution(mesh):
    in_specs = (
        P("expert", "tensor"),
        P("expert", None),
        P("expert", None),
        P("expert", "tensor", None),
        P("expert", "tensor", None),
        P("expert", None, "tensor"),
        P("expert", "tensor"),
    )
    out_specs = (
        P("expert", "tensor"),
        P("expert", "tensor"),
        P("expert", "tensor", None),
        P("expert", "tensor", None),
        P("expert", None, "tensor"),
    )
    body = functools.partial(local, mesh.shape["expert"], mesh.shape["tensor"] // 2)
    return jax.shard_map(body, mesh=mesh, in_specs=in_specs, out_specs=out_specs, check_vma=False)
```
